32 devices in a mesh: group: 4 (over x, core), site: 8 (over z, y).
Axes of the slice: x: 2, y: 2, z: 4, core: 2. Of those that a mesh axis runs over, the one named last changes fastest.
Arguments:
- residual_in: bfloat16 [8, 64, 128, 128], P('site', 'group'), may hold values from -6 to 6
- self_block: bfloat16 [8, 64, 64, 128], P('site'), may hold values from -0.25 to 0.25
- hop_blocks: bfloat16 [8, 64, 8, 64, 128], P('site'), may hold values from -0.1875 to 0.1875
Outputs:
- correction: float32 [8, 64, 128, 128], P('site', 'group')
- residual_out: float32 [8, 64, 128, 128], P('site', 'group')
The draws below stay inside these ranges and needn't reach their ends.
All inputs are finite; a program needn't handle non-finite values.
Results may differ from the reference program's by a relative error of at most 0.017.
Values may be sent and summed in bfloat16 or wider, within the bound.
No kernel may reach another device: no remote copies, remote signals or barrier semaphores. Data moves between devices by JAX's collectives and lax.ppermute only.
A program may use at most 64 MiB of HBM per device.

```python
import jax
import jax.numpy as jnp
from jax import lax

C = 64
RHS = 128
LY = 4
LZ = 2
STEPS = 4
X = 8
SPATIAL = 64
NT = 8


def levels(own_key, shape, split, low, high):
    def one(axis_at, blocks):
        steps = jax.random.uniform(jax.random.fold_in(jax.random.fold_in(own_key, 6), axis_at), (blocks,), jnp.float32, low / len(split), high / len(split))
        return jnp.repeat(jnp.exp(steps), shape[axis_at] // blocks).reshape((-1,) + (1,) * (len(shape) - axis_at - 1))

    level = one(*split[0])
    for cut in split[1:]:
        level = level * one(*cut)
    return level


def gaussian(rng, extent, scale, bound, shards=(), kind=jnp.bfloat16):
    gain = levels(rng, extent, shards, -0.22, 0.18) if shards else 1.0
    values = jax.random.normal(rng, extent, jnp.float32) * scale * gain
    return jnp.minimum(jnp.maximum(values, -bound), bound).astype(kind)


def setup_inputs(seed: int = 0) -> dict:
    arg_keys = jax.random.split(jax.random.key(seed), 4)
    return {
        "residual_in": gaussian(arg_keys[0], (NT, SPATIAL, RHS, 2 * C), 1.0, 6.0, ((0, 8), (1, 4))),
        "self_block": gaussian(arg_keys[1], (NT, SPATIAL, C, 2 * C), (8 * C) ** -0.5, 0.25, ((0, 8),)),
        "hop_blocks": gaussian(arg_keys[2], (NT, SPATIAL, 8, C, 2 * C), (14 * C) ** -0.5, 0.1875, ((0, 8),)),
    }


diagonal_shift = 1.5
center_value = 1.5
half_width = 1.0


def paired(vector):
    half = vector.shape[-1] // 2
    real_part = vector[..., :half]
    imag_part = vector[..., half:]
    conjugate = jnp.concatenate([real_part, -imag_part], axis=-1)
    swapped = jnp.concatenate([imag_part, real_part], axis=-1)
    return jnp.concatenate([conjugate, swapped], axis=-2)


def operate(vector, self_block, hop_blocks):
    grid = vector.reshape(NT, X, LY, LZ, RHS, 2 * C)
    moved = []
    for axis_number in (1, 2, 3, 0):
        moved.append(jnp.roll(grid, -1, axis_number).reshape(NT, SPATIAL, RHS, 2 * C))
        moved.append(jnp.roll(grid, 1, axis_number).reshape(NT, SPATIAL, RHS, 2 * C))
    stacked = jnp.stack(moved, axis=2)

    def one_slice(items):
        own, around, self_part, hop_part = items
        own_out = jnp.einsum('sab,skb->ska', self_part.astype(jnp.float32), paired(own).astype(jnp.float32))
        hop_out = jnp.einsum('smab,smkb->ska', hop_part.astype(jnp.float32), paired(around).astype(jnp.float32))
        total = own_out + hop_out
        return jnp.concatenate([total[:, :RHS], total[:, RHS:]], axis=-1)

    applied = lax.map(one_slice, (vector, stacked, self_block, hop_blocks))
    return diagonal_shift * vector.astype(jnp.float32) + applied


def reference(residual_in, self_block, hop_blocks):
    residual = residual_in.astype(jnp.float32)
    correction = jnp.zeros(residual.shape, jnp.float32)
    ratio = half_width / center_value
    direction = residual / center_value
    for number in range(STEPS):
        if number > 0:
            ratio_next = 1.0 / (2.0 * center_value / half_width - ratio)
            direction = ratio_next * ratio * direction + (2.0 * ratio_next / half_width) * residual
            ratio = ratio_next
        correction = correction + direction
        residual = residual - operate(direction.astype(jnp.bfloat16), self_block, hop_blocks)
    return correction, residual
```

```python
import functools

import jax
import jax.numpy as jnp
from jax import lax
from jax.experimental import pallas as pl
from jax.experimental.pallas import tpu as pltpu
from jax.sharding import PartitionSpec as P

LY = 4
LZ = 2
STEPS = 4
PIECES = 2

diagonal_shift = 1.5
center_value = 1.5
half_width = 1.0

WHOLE = pl.BlockSpec(memory_space=pltpu.VMEM)
VMEM_LIMIT = 32 * 1024 * 1024


def in_vmem(value):
    return pltpu.with_memory_space_constraint(value, pltpu.VMEM)


def coefficients():
    ratio = half_width / center_value
    out = []
    for _ in range(STEPS - 1):
        ratio_next = 1.0 / (2.0 * center_value / half_width - ratio)
        out.append((ratio_next * ratio, 2.0 * ratio_next / half_width))
        ratio = ratio_next
    return out


def call(kernel, outs, operands, flops, name, aliases=None, out_specs=None, in_specs=None, grid=()):
    nbytes = sum(o.size * o.dtype.itemsize for o in operands)
    in_specs = in_specs or [WHOLE] * len(operands)
    out_specs = out_specs or [WHOLE] * len(outs)
    operands = [in_vmem(o) if s is WHOLE else o for o, s in zip(operands, in_specs)]
    return pl.pallas_call(
        kernel,
        out_shape=outs,
        grid=grid,
        in_specs=in_specs,
        out_specs=out_specs,
        input_output_aliases=aliases or {},
        compiler_params=pltpu.CompilerParams(vmem_limit_bytes=VMEM_LIMIT),
        cost_estimate=pl.CostEstimate(flops=flops, bytes_accessed=nbytes, transcendentals=0),
        name=name,
    )(*operands)


def real_form(block):
    block = block.astype(jnp.float32)
    half = block.shape[-1] // 2
    lane = lax.broadcasted_iota(jnp.int32, block.shape, 1)
    upper = jnp.where(lane < half, block, -block)
    lower = pltpu.roll(block, half, 1)
    return jnp.concatenate([upper, lower], axis=0)


def prep_kernel(plane_sites, place, self_ref, hop_ref, local_ref, time_ref):
    parity = place[1]
    per = self_ref.shape[1]
    width = self_ref.shape[3]
    step = pl.program_id(0)
    for j in range(per):
        site = step * per + j
        plane = site // plane_sites
        hop = lambda m: real_form(hop_ref[0, j, m])
        parts = [
            real_form(self_ref[0, j]),
            hop(plane),
            hop(2),
            hop(3),
            hop(4) + hop(5),
            hop(1 - plane),
        ]
        for k, part in enumerate(parts):
            local_ref[site, :, k * width : (k + 1) * width] = part.astype(jnp.bfloat16)
        time_ref[site, :, :width] = hop(6 + parity).astype(jnp.bfloat16)
        time_ref[site, :, width:] = hop(7 - parity).astype(jnp.bfloat16)


def prep(self_block, hop_blocks, sites, plane_sites):
    place = jnp.stack([lax.axis_index("group"), lax.axis_index("site") % 2]).astype(jnp.int32)
    comps, width = self_block.shape[2:]
    per = 2
    grid_spec = pltpu.PrefetchScalarGridSpec(
        num_scalar_prefetch=1,
        grid=(sites // per,),
        in_specs=[
            pl.BlockSpec((1, per, comps, width), lambda i, p: (0, p[0] * (sites // per) + i, 0, 0)),
            pl.BlockSpec(
                (1, per, 8, comps, width), lambda i, p: (0, p[0] * (sites // per) + i, 0, 0, 0)
            ),
        ],
        out_specs=[WHOLE, WHOLE],
    )
    return pl.pallas_call(
        functools.partial(prep_kernel, plane_sites),
        out_shape=[
            pltpu.VMEM((sites, width, 6 * width), jnp.bfloat16),
            pltpu.VMEM((sites, width, 2 * width), jnp.bfloat16),
        ],
        grid_spec=grid_spec,
        compiler_params=pltpu.CompilerParams(vmem_limit_bytes=VMEM_LIMIT),
        name="prep",
    )(place, self_block, hop_blocks)


def times(vector, weight):
    return lax.dot_general(
        vector, weight, (((1,), (1,)), ((), ())), preferred_element_type=jnp.float32
    )


def local_kernel(plane, plane_sites, pieces, first, *refs):
    sent = refs[:pieces]
    halo, residual, weight = refs[pieces : pieces + 3]
    per = sent[0].shape[0]

    def at(site):
        return sent[site // per][site % per]

    acc = refs[pieces + 3]
    base = plane * plane_sites
    for s in range(plane_sites):
        y, z = s // LZ, s % LZ
        own = at(base + s)
        around = jnp.concatenate(
            [
                own,
                at((1 - plane) * plane_sites + s),
                at(base + (y + 1) % LY * LZ + z),
                at(base + (y - 1) % LY * LZ + z),
                at(base + y * LZ + 1 - z),
                halo[s],
            ],
            axis=1,
        )
        now = residual[0, base + s].astype(jnp.float32) if first else residual[s]
        acc[s] = now - diagonal_shift * own.astype(jnp.float32) - times(around, weight[base + s])


def time_kernel(offset, mode, scale, *refs):
    if mode == "last":
        acc, partner, other, weight, out = refs[:4] + refs[-1:]
    else:
        acc, partner, other, weight, direction, correction = refs[:6]
        out, direction_out, correction_out, sent_out = refs[6:]
    per = partner.shape[0]
    plane_offset = offset % acc.shape[0]
    for s in range(per):
        around = jnp.concatenate([partner[s], other[s]], axis=1)
        now = acc[plane_offset + s] - times(around, weight[offset + s])
        out[s] = now
        if mode != "last":
            if mode == "first":
                old = direction[0, offset + s].astype(jnp.float32) * (half_width / center_value)
                total = old
            else:
                old = direction[s]
                total = correction[s]
            new = scale[0] * old + scale[1] * now
            direction_out[s] = new
            correction_out[s] = total + new
            sent_out[s] = new.astype(jnp.bfloat16)


def body(residual_in, self_block, hop_blocks):
    _, sites, count, width = residual_in.shape
    plane_sites = LY * LZ
    groups, slices = lax.axis_size("group"), lax.axis_size("site")
    assert sites == 2 * plane_sites and slices % 2 == 0
    per = sites // PIECES
    per_plane = PIECES // 2
    swap = [(i, i ^ 1) for i in range(slices)]
    relay = [(i, (i + 2 - 4 * (i % 2)) % slices) for i in range(slices)]
    up = [(i, (i + 1) % groups) for i in range(groups)]
    down = [(j, i) for i, j in up]

    weight_local, weight_time = prep(self_block, hop_blocks, sites, plane_sites)
    scales = coefficients()
    block = (count, width)
    f32, bf16 = jnp.float32, jnp.bfloat16

    start = (residual_in[0].astype(f32) * (half_width / center_value)).astype(bf16)
    sent = [start[i * per : (i + 1) * per] for i in range(PIECES)]
    residual = [None] * PIECES
    direction = [None] * PIECES
    correction = [None] * PIECES
    mac = 2 * count * width * width
    for number in range(STEPS):
        halo = []
        for plane, pairs in ((0, up), (1, down)):
            far = sent[(1 - plane) * per_plane : (2 - plane) * per_plane]
            far = far[0] if per_plane == 1 else jnp.concatenate(far, axis=0)
            halo.append(lax.ppermute(far, "group", pairs))
        partner = [lax.ppermute(v, "site", swap) for v in sent]
        other = [lax.ppermute(v, "site", relay) for v in partner]
        acc = []
        for plane in range(2):
            if number == 0:
                now = residual_in
            else:
                now = residual[plane * per_plane : (plane + 1) * per_plane]
                now = now[0] if per_plane == 1 else jnp.concatenate(now, axis=0)
            acc.append(
                call(
                    functools.partial(local_kernel, plane, plane_sites, PIECES, number == 0),
                    [pltpu.VMEM((plane_sites,) + block, f32)],
                    [*sent, halo[plane], now, weight_local],
                    plane_sites * 6 * mac,
                    "local_terms",
                )[0]
            )
        last = number == STEPS - 1
        result = None
        new_sent = []
        for i in range(PIECES):
            mode = "first" if number == 0 else "last" if last else "middle"
            operands = [acc[i // per_plane], partner[i], other[i], weight_time]
            flops = per * 2 * mac
            kernel = functools.partial(
                time_kernel, i * per, mode, None if last else scales[number]
            )
            if last:
                spec = pl.BlockSpec((per,) + block, lambda _, i=i: (i, 0, 0))
                extra = [] if result is None else [result]
                result = call(
                    kernel,
                    [jax.ShapeDtypeStruct((sites,) + block, f32)],
                    operands + extra,
                    flops,
                    "time_terms_last",
                    aliases={4: 0} if extra else None,
                    grid=(1,),
                    out_specs=[spec],
                    in_specs=[WHOLE] * 4 + [pl.BlockSpec(memory_space=pltpu.HBM)] * len(extra),
                )[0]
                continue
            old = [residual_in, residual_in] if number == 0 else [direction[i], correction[i]]
            residual[i], direction[i], correction[i], new = call(
                kernel,
                [pltpu.VMEM((per,) + block, f32)] * 3 + [pltpu.VMEM((per,) + block, bf16)],
                operands + old,
                flops,
                "time_terms",
            )
            new_sent.append(new)
        sent = new_sent
    correction = jnp.concatenate(correction, axis=0)
    return correction[None], result[None]


def solution(mesh):
    return jax.shard_map(
        body,
        mesh=mesh,
        in_specs=(
            P("site", "group", None, None),
            P("site", None, None, None),
            P("site", None, None, None, None),
        ),
        out_specs=(P("site", "group", None, None), P("site", "group", None, None)),
        check_vma=False,
    )
```

```python
import functools

import jax
import jax.numpy as jnp
from jax import lax
from jax.experimental import pallas as pl
from jax.experimental.pallas import tpu as pltpu
from jax.sharding import PartitionSpec as P

LY = 4
LZ = 2
STEPS = 4
PIECES = 2

diagonal_shift = 1.5
center_value = 1.5
half_width = 1.0

F32, BF16 = jnp.float32, jnp.bfloat16
WHOLE = pl.BlockSpec(memory_space=pltpu.VMEM)
VMEM_LIMIT = 32 * 1024 * 1024


def coefficients():
    ratio = half_width / center_value
    out = []
    for _ in range(STEPS - 1):
        ratio_next = 1.0 / (2.0 * center_value / half_width - ratio)
        out.append((ratio_next * ratio, 2.0 * ratio_next / half_width))
        ratio = ratio_next
    return out


def call(kernel, outs, operands, flops, name, aliases=None, out_specs=None, in_specs=None, scratch=()):
    nbytes = sum(o.size * o.dtype.itemsize for o in operands)
    in_specs = in_specs or [WHOLE] * len(operands)
    out_specs = out_specs or [WHOLE] * len(outs)
    operands = [
        pltpu.with_memory_space_constraint(o, pltpu.VMEM) if s is WHOLE else o
        for o, s in zip(operands, in_specs)
    ]
    return pl.pallas_call(
        kernel,
        out_shape=outs,
        in_specs=in_specs,
        out_specs=out_specs,
        input_output_aliases=aliases or {},
        scratch_shapes=scratch,
        compiler_params=pltpu.CompilerParams(vmem_limit_bytes=VMEM_LIMIT),
        cost_estimate=pl.CostEstimate(flops=flops, bytes_accessed=nbytes, transcendentals=0),
        name=name,
    )(*operands)


def real_form(block):
    block = block.astype(F32)
    half = block.shape[-1] // 2
    lane = lax.broadcasted_iota(jnp.int32, block.shape, 1)
    upper = jnp.where(lane < half, block, -block)
    lower = pltpu.roll(block, half, 1)
    return jnp.concatenate([upper, lower], axis=0)


def gather_kernel(hop_hbm, out, sem):
    sites = out.shape[0]
    base = pl.multiple_of(lax.axis_index("group") * sites, sites)
    copy = pltpu.make_async_copy(hop_hbm.at[0, pl.ds(base, sites), pl.ds(6, 2)], out, sem)
    copy.start()
    copy.wait()


def gather_time(hop_blocks, sites):
    comps, width = hop_blocks.shape[3:]
    return call(
        gather_kernel,
        [pltpu.VMEM((sites, 2, comps, width), BF16)],
        [pltpu.with_memory_space_constraint(hop_blocks, pltpu.HBM)],
        0,
        "time_blocks",
        in_specs=[pl.BlockSpec(memory_space=pltpu.HBM)],
        scratch=[pltpu.SemaphoreType.DMA],
    )[0]


def prep_time_kernel(blocks, time_ref):
    sites, width = time_ref.shape[:2]
    parity = (lax.axis_index("site") + lax.axis_index("group")) % 2
    for site in range(sites):
        time_ref[site, :, :width] = real_form(blocks[site, parity]).astype(BF16)
        time_ref[site, :, width:] = real_form(blocks[site, 1 - parity]).astype(BF16)


def prep_kernel(plane_sites, batch, self_hbm, hop_hbm, local_ref, self_ref, hop_ref, sems):
    sites, width = local_ref.shape[:2]
    base = pl.multiple_of(lax.axis_index("group") * sites, sites)
    copies = []
    for i in range(sites // batch):
        there, here = pl.ds(base + i * batch, batch), pl.ds(i * batch, batch)
        copies.append(
            (
                pltpu.make_async_copy(
                    hop_hbm.at[0, there, pl.ds(0, 6)], hop_ref.at[here], sems.at[0, i]
                ),
                pltpu.make_async_copy(self_hbm.at[0, there], self_ref.at[here], sems.at[1, i]),
            )
        )
        for copy in copies[i]:
            copy.start()
    for site in range(sites):
        if site % batch == 0:
            for copy in copies[site // batch]:
                copy.wait()
        plane = site // plane_sites
        hop = lambda m: real_form(hop_ref[site, m])
        parts = [
            real_form(self_ref[site]),
            hop(plane),
            hop(2),
            hop(3),
            hop(4) + hop(5),
            hop(1 - plane),
        ]
        for k, part in enumerate(parts):
            local_ref[site, :, k * width : (k + 1) * width] = part.astype(BF16)


def prep(self_block, hop_blocks, sites, plane_sites):
    comps, width = self_block.shape[2:]
    batch = 2
    in_hbm = pl.BlockSpec(memory_space=pltpu.HBM)
    return call(
        functools.partial(prep_kernel, plane_sites, batch),
        [pltpu.VMEM((sites, width, 6 * width), BF16)],
        [
            pltpu.with_memory_space_constraint(self_block, pltpu.HBM),
            pltpu.with_memory_space_constraint(hop_blocks, pltpu.HBM),
        ],
        0,
        "prep",
        in_specs=[in_hbm, in_hbm],
        scratch=[
            pltpu.VMEM((sites, comps, width), BF16),
            pltpu.VMEM((sites, 6, comps, width), BF16),
            pltpu.SemaphoreType.DMA((2, sites // batch)),
        ],
    )[0]


def times(vector, weight):
    return lax.dot_general(
        vector, weight, (((1,), (1,)), ((), ())), preferred_element_type=F32
    )


def store_edges(offset, size, plane_sites, sent_out, core_out, chip_out):
    odd = lax.axis_index("group") % 2
    for plane in range(2):
        low = max(offset, plane * plane_sites)
        high = min(offset + size, (plane + 1) * plane_sites)
        if low >= high:
            continue
        here = pl.ds(low - offset, high - low)
        there = pl.ds(low - plane * plane_sites, high - low)

        @pl.when(odd == 1 - plane)
        def _():
            core_out[there] = sent_out[here]

        @pl.when(odd == plane)
        def _():
            chip_out[there] = sent_out[here]


def init_kernel(offset, plane_sites, size, residual, *refs):
    sent_out, core_out, chip_out = refs[-3:]
    for s in range(size):
        new = residual[0, offset + s].astype(F32) * (half_width / center_value)
        sent_out[s] = new.astype(BF16)
    store_edges(offset, size, plane_sites, sent_out, core_out, chip_out)


def local_kernel(plane_sites, offsets, first, *refs):
    pieces = len(offsets) - 1
    sent = refs[:pieces]
    core_halo, chip_halo, weight = refs[pieces : pieces + 3]
    residual = refs[pieces + 3 : -1]
    acc = refs[-1]

    def at(of, site):
        piece = max(i for i in range(pieces) if offsets[i] <= site)
        return of[piece][site - offsets[piece]]

    odd = lax.axis_index("group") % 2
    for plane in range(2):
        base = plane * plane_sites
        by_core = odd == 1 - plane
        for s in range(plane_sites):
            y, z = s // LZ, s % LZ
            own = at(sent, base + s)
            around = jnp.concatenate(
                [
                    own,
                    at(sent, (1 - plane) * plane_sites + s),
                    at(sent, base + (y + 1) % LY * LZ + z),
                    at(sent, base + (y - 1) % LY * LZ + z),
                    at(sent, base + y * LZ + 1 - z),
                    jnp.where(by_core, core_halo[s], chip_halo[s]),
                ],
                axis=1,
            )
            now = residual[0][0, base + s].astype(F32) if first else at(residual, base + s)
            acc[base + s] = (
                now - diagonal_shift * own.astype(F32) - times(around, weight[base + s])
            )


def middle_kernel(offset, size, near, own, weight, out):
    odd = lax.axis_index("group") % 2

    @pl.when(odd == 0)
    def _():
        out[...] = near[...]

    @pl.when(odd == 1)
    def _():
        for s in range(size):
            around = jnp.concatenate([own[s], near[s]], axis=1)
            out[s] = times(around, weight[offset + s]).astype(BF16)


def time_kernel(offset, size, plane_sites, mode, scale, *refs):
    acc, near, far, weight = refs[:4]
    if mode == "last":
        whole, out, sems = refs[-3:]
        copies = [
            pltpu.make_async_copy(out.at[s], whole.at[0, offset + s], sems.at[s])
            for s in range(size)
        ]
    else:
        direction = refs[4]
        out, direction_out, sent_out, core_out, chip_out = refs[-5:]

    def finish(s, now):
        out[s] = now
        if mode == "last":
            return
        if mode == "first":
            old = direction[0, offset + s].astype(F32) * (half_width / center_value)
        else:
            old = direction[s]
        new = scale[0] * old + scale[1] * now
        direction_out[s] = new
        sent_out[s] = new.astype(BF16)

    odd = lax.axis_index("group") % 2

    @pl.when(odd == 0)
    def _():
        for s in range(size):
            around = jnp.concatenate([near[s], far[s]], axis=1)
            finish(s, acc[offset + s] - times(around, weight[offset + s]))

    @pl.when(odd == 1)
    def _():
        for s in range(size):
            finish(s, acc[offset + s] - far[s].astype(F32))

    if mode == "last":
        for copy in copies:
            copy.start()
        for copy in copies:
            copy.wait()
    else:
        store_edges(offset, size, plane_sites, sent_out, core_out, chip_out)


def sum_kernel(offsets, residual, *refs):
    out = refs[-1]
    pieces = len(offsets) - 1
    for i in range(pieces):
        for s in range(offsets[i + 1] - offsets[i]):
            site = offsets[i] + s
            total = residual[0, site].astype(F32) * (half_width / center_value)
            for k in range(STEPS - 1):
                total = total + refs[k * pieces + i][s]
            out[0, site] = total


def body(residual_in, self_block, hop_blocks):
    _, sites, count, width = residual_in.shape
    plane_sites = LY * LZ
    groups, slices = lax.axis_size("group"), lax.axis_size("site")
    assert sites == 2 * plane_sites and slices % 2 == 0 and groups % 2 == 0
    offsets = [-(-i * sites // PIECES) for i in range(PIECES + 1)]
    sizes = [b - a for a, b in zip(offsets, offsets[1:])]
    swap = lambda t: t ^ 1
    relay = lambda t: (t + 2 - 4 * (t % 2)) % slices
    shift = lambda t: (t - 2 + 4 * (t % 2)) % slices
    every = lambda even, odd: [
        (g * slices + t, g * slices + (odd if g % 2 else even)(t))
        for g in range(groups)
        for t in range(slices)
    ]
    exchange = every(lambda t: t, swap)
    first_hop, second_hop = every(swap, shift), every(relay, swap)
    axes = ("group", "site")
    cores = [(i, i ^ 1) for i in range(groups)]
    chips = [(i, (i - 1 + 2 * (i % 2)) % groups) for i in range(groups)]

    block = (count, width)
    mac = 2 * count * width * width
    scales = coefficients()
    edge = pltpu.VMEM((plane_sites,) + block, BF16)

    residual_in = pltpu.with_memory_space_constraint(residual_in, pltpu.VMEM)
    sent = [None] * PIECES
    edges = []
    for i in range(PIECES):
        sent[i], *edges = call(
            functools.partial(init_kernel, offsets[i], plane_sites, sizes[i]),
            [pltpu.VMEM((sizes[i],) + block, BF16), edge, edge],
            [residual_in, *edges],
            0,
            "first_direction",
            aliases={1: 1, 2: 2} if edges else None,
        )
    time_blocks = lax.ppermute(gather_time(hop_blocks, sites), axes, exchange)
    weight_time = call(
        prep_time_kernel, [pltpu.VMEM((sites, width, 2 * width), BF16)], [time_blocks], 0, "prep_time"
    )[0]
    weight_local = prep(self_block, hop_blocks, sites, plane_sites)
    residual = [residual_in]
    direction = [residual_in] * PIECES
    directions = []
    for number in range(STEPS):
        first, last = number == 0, number == STEPS - 1
        near = [lax.ppermute(v, axes, first_hop) for v in sent]
        core_halo = lax.ppermute(edges[0], "group", cores)
        chip_halo = lax.ppermute(edges[1], "group", chips)
        far = [
            lax.ppermute(
                call(
                    functools.partial(middle_kernel, offsets[i], sizes[i]),
                    [pltpu.VMEM((sizes[i],) + block, BF16)],
                    [near[i], sent[i], weight_time],
                    sizes[i] * 2 * mac,
                    "second_message",
                )[0],
                axes,
                second_hop,
            )
            for i in range(PIECES)
        ]
        acc = call(
            functools.partial(local_kernel, plane_sites, offsets, first),
            [pltpu.VMEM((sites,) + block, F32)],
            [*sent, core_halo, chip_halo, weight_local, *residual],
            sites * 6 * mac,
            "local_terms",
        )[0]
        mode = "first" if first else "last" if last else "middle"
        edges = []
        result = []
        residual = [None] * PIECES
        if last:
            correction = call(
                functools.partial(sum_kernel, offsets),
                [jax.ShapeDtypeStruct((1, sites) + block, F32)],
                [residual_in, *sum(directions, [])],
                0,
                "correction",
            )[0]
        for i in range(PIECES):
            scale = None if last else scales[number]
            kernel = functools.partial(
                time_kernel, offsets[i], sizes[i], plane_sites, mode, scale
            )
            operands = [acc, near[i], far[i], weight_time]
            flops = sizes[i] * 2 * mac
            if last:
                in_hbm = pl.BlockSpec(memory_space=pltpu.HBM)
                result = call(
                    kernel,
                    [jax.ShapeDtypeStruct((1, sites) + block, F32)],
                    [*operands, *result],
                    flops,
                    "time_terms_last",
                    aliases={4: 0} if result else None,
                    in_specs=[WHOLE] * 4 + [in_hbm] * len(result),
                    out_specs=[in_hbm],
                    scratch=[
                        pltpu.VMEM((sizes[i],) + block, F32),
                        pltpu.SemaphoreType.DMA((sizes[i],)),
                    ],
                )
                continue
            piece = lambda kind: pltpu.VMEM((sizes[i],) + block, kind)
            residual[i], direction[i], sent[i], *edges = call(
                kernel,
                [piece(F32), piece(F32), piece(BF16), edge, edge],
                operands + [direction[i], *edges],
                flops,
                "time_terms",
                aliases={5: 3, 6: 4} if edges else None,
            )
        directions.append(list(direction))
    return correction, result[0]


def solution(mesh):
    return jax.shard_map(
        body,
        mesh=mesh,
        in_specs=(
            P("site", "group", None, None),
            P("site", None, None, None),
            P("site", None, None, None, None),
        ),
        out_specs=(P("site", "group", None, None), P("site", "group", None, None)),
        check_vma=False,
    )
```

```python
import functools

import jax
import jax.numpy as jnp
from jax import lax
from jax.experimental import pallas as pl
from jax.experimental.pallas import tpu as pltpu
from jax.sharding import PartitionSpec as P

LY = 4
LZ = 2
STEPS = 4
PLANE = LY * LZ

diagonal_shift = 1.5
center_value = 1.5
half_width = 1.0

F32, BF16 = jnp.float32, jnp.bfloat16
WHOLE = pl.BlockSpec(memory_space=pltpu.VMEM)
IN_HBM = pl.BlockSpec(memory_space=pltpu.HBM)
VMEM_LIMIT = 32 * 1024 * 1024


def coefficients():
    ratio = half_width / center_value
    out = []
    for _ in range(STEPS - 1):
        ratio_next = 1.0 / (2.0 * center_value / half_width - ratio)
        out.append((ratio_next * ratio, 2.0 * ratio_next / half_width))
        ratio = ratio_next
    return out


def call(kernel, outs, operands, flops, name, aliases=None, out_specs=None, in_specs=None, scratch=()):
    nbytes = sum(o.size * o.dtype.itemsize for o in operands)
    in_specs = in_specs or [WHOLE] * len(operands)
    out_specs = out_specs or [WHOLE] * len(outs)
    operands = [
        pltpu.with_memory_space_constraint(o, pltpu.VMEM if s is WHOLE else pltpu.HBM)
        for o, s in zip(operands, in_specs)
    ]
    return pl.pallas_call(
        kernel,
        out_shape=outs,
        in_specs=in_specs,
        out_specs=out_specs,
        input_output_aliases=aliases or {},
        scratch_shapes=scratch,
        compiler_params=pltpu.CompilerParams(vmem_limit_bytes=VMEM_LIMIT),
        cost_estimate=pl.CostEstimate(flops=flops, bytes_accessed=nbytes, transcendentals=0),
        name=name,
    )(*operands)


def odd_group():
    return lax.axis_index("group") % 2


def plane_of(piece):
    return (piece + odd_group()) % 2


def plane_sites(piece):
    return pl.ds(pl.multiple_of(plane_of(piece) * PLANE, PLANE), PLANE)


def real_form(block):
    block = block.astype(F32)
    half = block.shape[-1] // 2
    lane = lax.broadcasted_iota(jnp.int32, block.shape, 1)
    upper = jnp.where(lane < half, block, -block)
    lower = pltpu.roll(block, half, 1)
    return jnp.concatenate([upper, lower], axis=0)


def prep_kernel(batch, self_hbm, hop_hbm, *refs):
    local_refs, time_refs, (self_ref, hop_ref, sems) = refs[:2], refs[2:4], refs[4:]
    sites = hop_ref.shape[0]
    width = local_refs[0].shape[1]
    parity = lax.axis_index("site") % 2
    copies = []
    for i in range(sites // batch):
        piece, offset = divmod(i * batch, PLANE)
        base = lax.axis_index("group") * sites + plane_of(piece) * PLANE + offset
        there, here = pl.ds(pl.multiple_of(base, batch), batch), pl.ds(i * batch, batch)
        copies.append(
            (
                pltpu.make_async_copy(hop_hbm.at[0, there], hop_ref.at[here], sems.at[0, i]),
                pltpu.make_async_copy(self_hbm.at[0, there], self_ref.at[here], sems.at[1, i]),
            )
        )
        for copy in copies[i]:
            copy.start()
    for site in range(sites):
        if site % batch == 0:
            for copy in copies[site // batch]:
                copy.wait()
        piece, own = divmod(site, PLANE)
        plane = plane_of(piece)
        hop = lambda m: real_form(hop_ref[site, m])
        parts = [
            real_form(self_ref[site]),
            hop(plane),
            hop(2),
            hop(3),
            hop(4) + hop(5),
            hop(1 - plane),
        ]
        for k, part in enumerate(parts):
            local_refs[piece][own, :, k * width : (k + 1) * width] = part.astype(BF16)
        time_refs[piece][own, :, :width] = hop(6 + parity).astype(BF16)
        time_refs[piece][own, :, width:] = hop(7 - parity).astype(BF16)


def prep(self_block, hop_blocks, sites):
    comps, width = self_block.shape[2:]
    batch = 2
    weight = lambda parts: pltpu.VMEM((PLANE, width, parts * width), BF16)
    outs = call(
        functools.partial(prep_kernel, batch),
        [weight(6)] * 2 + [weight(2)] * 2,
        [self_block, hop_blocks],
        0,
        "prep",
        in_specs=[IN_HBM, IN_HBM],
        scratch=[
            pltpu.VMEM((sites, comps, width), BF16),
            pltpu.VMEM((sites, 8, comps, width), BF16),
            pltpu.SemaphoreType.DMA((2, sites // batch)),
        ],
    )
    return outs[:2], outs[2:4]


def times(vector, weight):
    return lax.dot_general(
        vector, weight, (((1,), (1,)), ((), ())), preferred_element_type=F32
    )


def first_kernel(piece, residual_hbm, *refs):
    residual, sent_out, sems = refs[-3:]
    base = plane_of(piece) * PLANE
    copies = [
        pltpu.make_async_copy(residual_hbm.at[0, base + s], residual.at[s], sems.at[s])
        for s in range(PLANE)
    ]
    for copy in copies:
        copy.start()
    for s in range(PLANE):
        copies[s].wait()
        sent_out[s] = (residual[s].astype(F32) * (half_width / center_value)).astype(BF16)


def local_kernel(this, that, halo, weight, residual, acc):
    for s in range(PLANE):
        y, z = s // LZ, s % LZ
        own = this[s]
        around = jnp.concatenate(
            [
                own,
                that[s],
                this[(y + 1) % LY * LZ + z],
                this[(y - 1) % LY * LZ + z],
                this[y * LZ + 1 - z],
                halo[s],
            ],
            axis=1,
        )
        acc[s] = (
            residual[s].astype(F32) - diagonal_shift * own.astype(F32) - times(around, weight[s])
        )


def time_kernel(piece, mode, scale, *refs):
    acc, near, far, weight = refs[:4]
    if mode == "last":
        whole, out, sems = refs[-3:]
        base = plane_of(piece) * PLANE
        copies = [
            pltpu.make_async_copy(out.at[s], whole.at[0, base + s], sems.at[s]) for s in range(PLANE)
        ]
    else:
        direction = refs[4]
        out, direction_out, sent_out = refs[-3:]

    for s in range(PLANE):
        around = jnp.concatenate([near[s], far[s]], axis=1)
        now = acc[s] - times(around, weight[s])
        out[s] = now
        if mode == "last":
            copies[s].start()
            continue
        old = direction[s].astype(F32)
        if mode == "first":
            old = old * (half_width / center_value)
        new = scale[0] * old + scale[1] * now
        direction_out[s] = new
        sent_out[s] = new.astype(BF16)
    if mode == "last":
        for copy in copies:
            copy.wait()


def sum_kernel(residual_a, residual_b, *refs):
    out = refs[-1]
    for piece, residual in enumerate((residual_a, residual_b)):
        total = residual[...].astype(F32) * (half_width / center_value)
        for ref in refs[piece:-1:2]:
            total = total + ref[...]
        out[0, plane_sites(piece)] = total


def body(residual_in, self_block, hop_blocks):
    _, sites, count, width = residual_in.shape
    groups, slices = lax.axis_size("group"), lax.axis_size("site")
    assert sites == 2 * PLANE and slices % 2 == 0 and groups % 2 == 0
    swap = [(t, t ^ 1) for t in range(slices)]
    relay = [(t, (t + 2 - 4 * (t % 2)) % slices) for t in range(slices)]
    cores = [(i, i ^ 1) for i in range(groups)]
    chips = [(i, (i - 1 + 2 * (i % 2)) % groups) for i in range(groups)]

    block = (count, width)
    piece = lambda kind: pltpu.VMEM((PLANE,) + block, kind)
    whole = jax.ShapeDtypeStruct((1, sites) + block, F32)
    flops = 2 * PLANE * count * width * width
    scales = coefficients()

    weight_local, weight_time = prep(self_block, hop_blocks, sites)
    start, sent = zip(
        *[
            call(
                functools.partial(first_kernel, i),
                [piece(BF16), piece(BF16)],
                [residual_in] + [weight_local[0]] * i,
                0,
                "first_direction",
                in_specs=[IN_HBM] + [WHOLE] * i,
                scratch=[pltpu.SemaphoreType.DMA((PLANE,))],
            )
            for i in range(2)
        ]
    )
    residual, direction = start, start
    directions = []
    for number in range(STEPS):
        first, last = number == 0, number == STEPS - 1
        near = [lax.ppermute(v, "site", swap) for v in sent]
        halo = [lax.ppermute(sent[0], "group", chips), lax.ppermute(sent[1], "group", cores)]
        far = [lax.ppermute(v, "site", relay) for v in near]
        acc = [
            call(
                local_kernel,
                [piece(F32)],
                [sent[i], sent[1 - i], halo[i], weight_local[i], residual[i]],
                6 * flops,
                "local_terms",
            )[0]
            for i in range(2)
        ]
        operands = lambda i: [acc[i], near[i], far[i], weight_time[i]]
        if last:
            correction = call(sum_kernel, [whole], [*start, *sum(directions, ())], 0, "correction")[0]
            result = []
            for i in range(2):
                result = call(
                    functools.partial(time_kernel, i, "last", None),
                    [whole],
                    [*operands(i), *result],
                    2 * flops,
                    "time_terms_last",
                    aliases={4: 0} if result else None,
                    in_specs=[WHOLE] * 4 + [IN_HBM] * len(result),
                    out_specs=[IN_HBM],
                    scratch=[piece(F32), pltpu.SemaphoreType.DMA((PLANE,))],
                )
            return correction, result[0]
        mode = "first" if first else "middle"
        residual, direction, sent = zip(
            *[
                call(
                    functools.partial(time_kernel, i, mode, scales[number]),
                    [piece(F32), piece(F32), piece(BF16)],
                    [*operands(i), direction[i]],
                    2 * flops,
                    "time_terms",
                )
                for i in range(2)
            ]
        )
        directions.append(direction)


def solution(mesh):
    return jax.shard_map(
        body,
        mesh=mesh,
        in_specs=(
            P("site", "group", None, None),
            P("site", None, None, None),
            P("site", None, None, None, None),
        ),
        out_specs=(P("site", "group", None, None), P("site", "group", None, None)),
        check_vma=False,
    )
```

```python
import functools

import jax
import jax.numpy as jnp
from jax import lax
from jax.experimental import pallas as pl
from jax.experimental.pallas import tpu as pltpu
from jax.sharding import PartitionSpec as P

LY = 4
LZ = 2
STEPS = 4
PLANE = LY * LZ

diagonal_shift = 1.5
center_value = 1.5
half_width = 1.0

F32, BF16 = jnp.float32, jnp.bfloat16
WHOLE = pl.BlockSpec(memory_space=pltpu.VMEM)
IN_HBM = pl.BlockSpec(memory_space=pltpu.HBM)
VMEM_LIMIT = 32 * 1024 * 1024


def coefficients():
    ratio = half_width / center_value
    out = []
    for _ in range(STEPS - 1):
        ratio_next = 1.0 / (2.0 * center_value / half_width - ratio)
        out.append((ratio_next * ratio, 2.0 * ratio_next / half_width))
        ratio = ratio_next
    return out


def call(kernel, outs, operands, flops, name, aliases=None, out_specs=None, in_specs=None, scratch=()):
    nbytes = sum(o.size * o.dtype.itemsize for o in operands)
    in_specs = in_specs or [WHOLE] * len(operands)
    out_specs = out_specs or [WHOLE] * len(outs)
    operands = [
        pltpu.with_memory_space_constraint(o, pltpu.VMEM if s is WHOLE else pltpu.HBM)
        for o, s in zip(operands, in_specs)
    ]
    return pl.pallas_call(
        kernel,
        out_shape=outs,
        in_specs=in_specs,
        out_specs=out_specs,
        input_output_aliases=aliases or {},
        scratch_shapes=scratch,
        compiler_params=pltpu.CompilerParams(vmem_limit_bytes=VMEM_LIMIT),
        cost_estimate=pl.CostEstimate(flops=flops, bytes_accessed=nbytes, transcendentals=0),
        name=name,
    )(*operands)


def odd_group():
    return lax.axis_index("group") % 2


def plane_of(piece):
    return (piece + odd_group()) % 2


def plane_sites(piece):
    return pl.ds(pl.multiple_of(plane_of(piece) * PLANE, PLANE), PLANE)


def real_form(block):
    block = block.astype(F32)
    half = block.shape[-1] // 2
    lane = lax.broadcasted_iota(jnp.int32, block.shape, 1)
    upper = jnp.where(lane < half, block, -block)
    lower = pltpu.roll(block, half, 1)
    return jnp.concatenate([upper, lower], axis=0)


def prep_kernel(batch, self_hbm, hop_hbm, *refs):
    local_refs, time_ref, (self_ref, hop_ref, sems) = refs[:2], refs[2], refs[3:]
    sites = hop_ref.shape[0]
    width = time_ref.shape[1]
    parity = lax.axis_index("site") % 2
    copies = []
    for i in range(sites // batch):
        piece, offset = divmod(i * batch, PLANE)
        base = lax.axis_index("group") * sites + plane_of(piece) * PLANE + offset
        there, here = pl.ds(pl.multiple_of(base, batch), batch), pl.ds(i * batch, batch)
        copies.append(
            (
                pltpu.make_async_copy(hop_hbm.at[0, there], hop_ref.at[here], sems.at[0, i]),
                pltpu.make_async_copy(self_hbm.at[0, there], self_ref.at[here], sems.at[1, i]),
            )
        )
        for copy in copies[i]:
            copy.start()
    for site in range(sites):
        if site % batch == 0:
            for copy in copies[site // batch]:
                copy.wait()
        piece, own = divmod(site, PLANE)
        plane = plane_of(piece)
        hop = lambda m: real_form(hop_ref[site, m])
        parts = [
            real_form(self_ref[site]),
            hop(plane),
            hop(2),
            hop(3),
            hop(4) + hop(5),
            hop(1 - plane),
        ]
        for k, part in enumerate(parts):
            local_refs[piece][own, :, k * width : (k + 1) * width] = part.astype(BF16)
        if piece == 1:
            time_ref[own, :, :width] = hop(6 + parity).astype(BF16)
            time_ref[own, :, width:] = hop(7 - parity).astype(BF16)


def prep(self_block, hop_blocks, sites):
    comps, width = self_block.shape[2:]
    batch = 2
    weight = lambda parts: pltpu.VMEM((PLANE, width, parts * width), BF16)
    outs = call(
        functools.partial(prep_kernel, batch),
        [weight(6), weight(6), weight(2)],
        [self_block, hop_blocks],
        0,
        "prep",
        in_specs=[IN_HBM, IN_HBM],
        scratch=[
            pltpu.VMEM((sites, comps, width), BF16),
            pltpu.VMEM((sites, 8, comps, width), BF16),
            pltpu.SemaphoreType.DMA((2, sites // batch)),
        ],
    )
    return outs[:2], outs[2]


def partner_kernel(blocks, time_ref):
    width = time_ref.shape[1]
    parity = (lax.axis_index("site") + 1) % 2
    for s in range(PLANE):
        time_ref[s, :, :width] = real_form(blocks[s, parity]).astype(BF16)
        time_ref[s, :, width:] = real_form(blocks[s, 1 - parity]).astype(BF16)


def middle_kernel(near, own, weight, *refs):
    out = refs[-1]
    for s in range(PLANE):
        around = jnp.concatenate([own[s], near[s]], axis=1)
        out[s] = times(around, weight[s]).astype(BF16)


def times(vector, weight):
    return lax.dot_general(
        vector, weight, (((1,), (1,)), ((), ())), preferred_element_type=F32
    )


def first_kernel(piece, sites, residual_hbm, other, *refs):
    base = plane_of(piece) * PLANE
    if piece == 0:
        residual, sent_out, blocks, sems, sem = refs
        there = pl.ds(pl.multiple_of(lax.axis_index("group") * sites + base, PLANE), PLANE)
        last = pltpu.make_async_copy(other.at[0, there, pl.ds(6, 2)], blocks, sem)
        last.start()
    else:
        residual, sent_out, sems = refs
    copies = [
        pltpu.make_async_copy(residual_hbm.at[0, base + s], residual.at[s], sems.at[s])
        for s in range(PLANE)
    ]
    for copy in copies:
        copy.start()
    for s in range(PLANE):
        copies[s].wait()
        sent_out[s] = (residual[s].astype(F32) * (half_width / center_value)).astype(BF16)
    if piece == 0:
        last.wait()


def local_kernel(this, that, halo, weight, residual, acc):
    for s in range(PLANE):
        y, z = s // LZ, s % LZ
        own = this[s]
        around = jnp.concatenate(
            [
                own,
                that[s],
                this[(y + 1) % LY * LZ + z],
                this[(y - 1) % LY * LZ + z],
                this[y * LZ + 1 - z],
                halo[s],
            ],
            axis=1,
        )
        acc[s] = (
            residual[s].astype(F32) - diagonal_shift * own.astype(F32) - times(around, weight[s])
        )


def time_kernel(piece, mode, scale, *refs):
    acc, far = refs[:2]
    if mode == "last":
        whole, out, sems = refs[-3:]
        base = plane_of(piece) * PLANE
        copies = [
            pltpu.make_async_copy(out.at[s], whole.at[0, base + s], sems.at[s]) for s in range(PLANE)
        ]
    else:
        direction = refs[2]
        out, direction_out, sent_out = refs[-3:]

    for s in range(PLANE):
        if piece == 1:
            near, weight = refs[-5:-3] if mode == "last" else refs[3:5]
            around = jnp.concatenate([near[s], far[s]], axis=1)
            now = acc[s] - times(around, weight[s])
        else:
            now = acc[s] - far[s].astype(F32)
        out[s] = now
        if mode == "last":
            copies[s].start()
            continue
        old = direction[s].astype(F32)
        if mode == "first":
            old = old * (half_width / center_value)
        new = scale[0] * old + scale[1] * now
        direction_out[s] = new
        sent_out[s] = new.astype(BF16)
    if mode == "last":
        for copy in copies:
            copy.wait()


def sum_kernel(residual_a, residual_b, *refs):
    out = refs[-1]
    for piece, residual in enumerate((residual_a, residual_b)):
        total = residual[...].astype(F32) * (half_width / center_value)
        for ref in refs[piece:-1:2]:
            total = total + ref[...]
        out[0, plane_sites(piece)] = total


def body(residual_in, self_block, hop_blocks):
    _, sites, count, width = residual_in.shape
    groups, slices = lax.axis_size("group"), lax.axis_size("site")
    assert sites == 2 * PLANE and slices % 2 == 0 and groups % 2 == 0
    swap = [(t, t ^ 1) for t in range(slices)]
    relay = [(t, (t + 2 - 4 * (t % 2)) % slices) for t in range(slices)]
    shift = [(b, a) for a, b in relay]
    cores = [(i, i ^ 1) for i in range(groups)]
    chips = [(i, (i - 1 + 2 * (i % 2)) % groups) for i in range(groups)]

    block = (count, width)
    piece = lambda kind: pltpu.VMEM((PLANE,) + block, kind)
    whole = jax.ShapeDtypeStruct((1, sites) + block, F32)
    flops = 2 * PLANE * count * width * width
    scales = coefficients()

    comps = width // 2
    weight_local, weight_time = prep(self_block, hop_blocks, sites)
    sems = pltpu.SemaphoreType.DMA((PLANE,))
    start_0, sent_0, blocks = call(
        functools.partial(first_kernel, 0, sites),
        [piece(BF16), piece(BF16), pltpu.VMEM((PLANE, 2, comps, width), BF16)],
        [residual_in, hop_blocks],
        0,
        "first_direction",
        in_specs=[IN_HBM] * 2,
        scratch=[sems, pltpu.SemaphoreType.DMA],
    )
    start_1, sent_1 = call(
        functools.partial(first_kernel, 1, sites),
        [piece(BF16), piece(BF16)],
        [residual_in, sent_0],
        0,
        "first_direction",
        in_specs=[IN_HBM, WHOLE],
        scratch=[sems],
    )
    start, sent = [start_0, start_1], [sent_0, sent_1]
    weight_partner = call(
        partner_kernel,
        [pltpu.VMEM((PLANE, width, 2 * width), BF16)],
        [lax.ppermute(blocks, "site", swap)],
        0,
        "partner_weights",
    )[0]
    residual, direction = start, start
    directions = []
    for number in range(STEPS):
        first, last = number == 0, number == STEPS - 1
        near = [lax.ppermute(sent[0], "site", shift), lax.ppermute(sent[1], "site", swap)]
        halo = [lax.ppermute(sent[0], "group", chips), lax.ppermute(sent[1], "group", cores)]
        terms = call(
            middle_kernel,
            [piece(BF16)],
            [near[0], sent[0], weight_partner] + ([weight_local[0]] if first else []),
            2 * flops,
            "partner_terms",
        )[0]
        far = [lax.ppermute(terms, "site", swap), lax.ppermute(near[1], "site", relay)]
        acc = [
            call(
                local_kernel,
                [piece(F32)],
                [sent[i], sent[1 - i], halo[i], weight_local[i], residual[i]],
                6 * flops,
                "local_terms",
            )[0]
            for i in range(2)
        ]
        operands = lambda i: [acc[i], far[i]]
        extra = [[], [near[1], weight_time]]
        if last:
            correction = call(sum_kernel, [whole], [*start, *sum(directions, ())], 0, "correction")[0]
            result = []
            for i in range(2):
                result = call(
                    functools.partial(time_kernel, i, "last", None),
                    [whole],
                    [*operands(i), *result, *extra[i]],
                    2 * flops,
                    "time_terms_last",
                    aliases={2: 0} if result else None,
                    in_specs=[WHOLE] * 2 + [IN_HBM] * len(result) + [WHOLE] * len(extra[i]),
                    out_specs=[IN_HBM],
                    scratch=[piece(F32), pltpu.SemaphoreType.DMA((PLANE,))],
                )
            return correction, result[0]
        mode = "first" if first else "middle"
        residual, direction, sent = zip(
            *[
                call(
                    functools.partial(time_kernel, i, mode, scales[number]),
                    [piece(F32), piece(F32), piece(BF16)],
                    [*operands(i), direction[i], *extra[i]],
                    2 * flops,
                    "time_terms",
                )
                for i in range(2)
            ]
        )
        directions.append(direction)


def solution(mesh):
    return jax.shard_map(
        body,
        mesh=mesh,
        in_specs=(
            P("site", "group", None, None),
            P("site", None, None, None),
            P("site", None, None, None, None),
        ),
        out_specs=(P("site", "group", None, None), P("site", "group", None, None)),
        check_vma=False,
    )
```

```python
import functools

import jax
import jax.numpy as jnp
from jax import lax
from jax.experimental import pallas as pl
from jax.experimental.pallas import tpu as pltpu
from jax.sharding import PartitionSpec as P

LY = 4
LZ = 2
STEPS = 4
PLANE = LY * LZ
PIECES = 3

diagonal_shift = 1.5
center_value = 1.5
half_width = 1.0

F32, BF16 = jnp.float32, jnp.bfloat16
WHOLE = pl.BlockSpec(memory_space=pltpu.VMEM)
IN_HBM = pl.BlockSpec(memory_space=pltpu.HBM)
VMEM_LIMIT = 32 * 1024 * 1024


def coefficients():
    ratio = half_width / center_value
    out = []
    for _ in range(STEPS - 1):
        ratio_next = 1.0 / (2.0 * center_value / half_width - ratio)
        out.append((ratio_next * ratio, 2.0 * ratio_next / half_width))
        ratio = ratio_next
    return out


def call(kernel, outs, operands, flops, name, aliases=None, out_specs=None, in_specs=None, scratch=()):
    nbytes = sum(o.size * o.dtype.itemsize for o in operands)
    in_specs = in_specs or [WHOLE] * len(operands)
    out_specs = out_specs or [WHOLE] * len(outs)
    operands = [
        pltpu.with_memory_space_constraint(o, pltpu.VMEM if s is WHOLE else pltpu.HBM)
        for o, s in zip(operands, in_specs)
    ]
    return pl.pallas_call(
        kernel,
        out_shape=outs,
        in_specs=in_specs,
        out_specs=out_specs,
        input_output_aliases=aliases or {},
        scratch_shapes=scratch,
        compiler_params=pltpu.CompilerParams(vmem_limit_bytes=VMEM_LIMIT),
        cost_estimate=pl.CostEstimate(flops=flops, bytes_accessed=nbytes, transcendentals=0),
        name=name,
    )(*operands)


def odd_group():
    return lax.axis_index("group") % 2


def plane_of(plane):
    return (plane + odd_group()) % 2


def place_of(site):
    return plane_of(site // PLANE) * PLANE + site % PLANE


def real_form(block):
    block = block.astype(F32)
    half = block.shape[-1] // 2
    lane = lax.broadcasted_iota(jnp.int32, block.shape, 1)
    upper = jnp.where(lane < half, block, -block)
    lower = pltpu.roll(block, half, 1)
    return jnp.concatenate([upper, lower], axis=0)


def prep_kernel(batch, self_hbm, hop_hbm, *refs):
    local_refs, time_refs, (self_ref, hop_ref, sems) = refs[:2], refs[2:4], refs[4:]
    sites = hop_ref.shape[0]
    width = local_refs[0].shape[1]
    parity = lax.axis_index("site") % 2
    copies = []
    for i in range(sites // batch):
        piece, offset = divmod(i * batch, PLANE)
        base = lax.axis_index("group") * sites + plane_of(piece) * PLANE + offset
        there, here = pl.ds(pl.multiple_of(base, batch), batch), pl.ds(i * batch, batch)
        copies.append(
            (
                pltpu.make_async_copy(hop_hbm.at[0, there], hop_ref.at[here], sems.at[0, i]),
                pltpu.make_async_copy(self_hbm.at[0, there], self_ref.at[here], sems.at[1, i]),
            )
        )
        for copy in copies[i]:
            copy.start()
    for site in range(sites):
        if site % batch == 0:
            for copy in copies[site // batch]:
                copy.wait()
        piece, own = divmod(site, PLANE)
        plane = plane_of(piece)
        hop = lambda m: real_form(hop_ref[site, m])
        parts = [
            real_form(self_ref[site]),
            hop(plane),
            hop(2),
            hop(3),
            hop(4) + hop(5),
            hop(1 - plane),
        ]
        for k, part in enumerate(parts):
            local_refs[piece][own, :, k * width : (k + 1) * width] = part.astype(BF16)
        time_refs[piece][own, :, :width] = hop(6 + parity).astype(BF16)
        time_refs[piece][own, :, width:] = hop(7 - parity).astype(BF16)


def prep(self_block, hop_blocks, sites):
    comps, width = self_block.shape[2:]
    batch = 2
    weight = lambda parts: pltpu.VMEM((PLANE, width, parts * width), BF16)
    outs = call(
        functools.partial(prep_kernel, batch),
        [weight(6)] * 2 + [weight(2)] * 2,
        [self_block, hop_blocks],
        0,
        "prep",
        in_specs=[IN_HBM, IN_HBM],
        scratch=[
            pltpu.VMEM((sites, comps, width), BF16),
            pltpu.VMEM((sites, 8, comps, width), BF16),
            pltpu.SemaphoreType.DMA((2, sites // batch)),
        ],
    )
    return outs[:2], outs[2:4]


def times(vector, weight):
    return lax.dot_general(
        vector, weight, (((1,), (1,)), ((), ())), preferred_element_type=F32
    )


def planes_in(piece):
    return sorted({site // PLANE for site in piece})


def store_edges(piece, sent_out, edges):
    for plane, edge in zip(planes_in(piece), edges):
        mine = [site for site in piece if site // PLANE == plane]
        edge[pl.ds(mine[0] % PLANE, len(mine))] = sent_out[pl.ds(mine[0] - piece[0], len(mine))]


def first_kernel(piece, residual_hbm, *refs):
    planes = len(planes_in(piece))
    residual, sent_out, *edges, sems = refs[-3 - planes :]
    copies = [
        pltpu.make_async_copy(residual_hbm.at[0, place_of(site)], residual.at[s], sems.at[s])
        for s, site in enumerate(piece)
    ]
    for copy in copies:
        copy.start()
    for s, copy in enumerate(copies):
        copy.wait()
        sent_out[s] = (residual[s].astype(F32) * (half_width / center_value)).astype(BF16)
    store_edges(piece, sent_out, edges)


def local_kernel(plane, pieces, halo, weight, *refs):
    count = len(pieces)
    sent, residual, acc = refs[:count], refs[count : 2 * count], refs[-1]

    def at(of, site):
        piece = max(i for i in range(count) if pieces[i][0] <= site)
        return of[piece][site - pieces[piece][0]]

    for s in range(PLANE):
        y, z = s // LZ, s % LZ
        here = lambda y, z: at(sent, plane * PLANE + y % LY * LZ + z)
        own = here(y, z)
        around = jnp.concatenate(
            [own, at(sent, (1 - plane) * PLANE + s), here(y + 1, z), here(y - 1, z), here(y, 1 - z), halo[s]],
            axis=1,
        )
        acc[s] = (
            at(residual, plane * PLANE + s).astype(F32)
            - diagonal_shift * own.astype(F32)
            - times(around, weight[s])
        )


def time_kernel(piece, mode, scale, *refs):
    planes = planes_in(piece)
    acc, weight = refs[: len(planes)], refs[len(planes) : 2 * len(planes)]
    near, far, *refs = refs[2 * len(planes) :]
    if mode == "last":
        whole, out, sems = refs[-3:]
        copies = [
            pltpu.make_async_copy(out.at[s], whole.at[0, place_of(site)], sems.at[s])
            for s, site in enumerate(piece)
        ]
    else:
        direction = refs[0]
        out, direction_out, sent_out, *edges = refs[-3 - len(planes) :]
    for s, site in enumerate(piece):
        plane = planes.index(site // PLANE)
        around = jnp.concatenate([near[s], far[s]], axis=1)
        now = acc[plane][site % PLANE] - times(around, weight[plane][site % PLANE])
        out[s] = now
        if mode == "last":
            copies[s].start()
            continue
        old = direction[s].astype(F32)
        if mode == "first":
            old = old * (half_width / center_value)
        new = scale[0] * old + scale[1] * now
        direction_out[s] = new
        sent_out[s] = new.astype(BF16)
    if mode == "last":
        for copy in copies:
            copy.wait()
    else:
        store_edges(piece, sent_out, edges)


def sum_kernel(pieces, *refs):
    out, count = refs[-1], len(pieces)
    for i, piece in enumerate(pieces):
        for s, site in enumerate(piece):
            total = refs[i][s].astype(F32) * (half_width / center_value)
            for ref in refs[i + count : -1 : count]:
                total = total + ref[s]
            out[0, place_of(site)] = total


def body(residual_in, self_block, hop_blocks):
    _, sites, count, width = residual_in.shape
    groups, slices = lax.axis_size("group"), lax.axis_size("site")
    assert sites == 2 * PLANE and slices % 2 == 0 and groups % 2 == 0
    swap = [(t, t ^ 1) for t in range(slices)]
    relay = [(t, (t + 2 - 4 * (t % 2)) % slices) for t in range(slices)]
    cores = [(i, i ^ 1) for i in range(groups)]
    chips = [(i, (i - 1 + 2 * (i % 2)) % groups) for i in range(groups)]

    block = (count, width)
    offsets = [-(-i * sites // PIECES) for i in range(PIECES + 1)]
    pieces = [tuple(range(a, b)) for a, b in zip(offsets, offsets[1:])]
    vector = lambda piece, kind: pltpu.VMEM((len(piece),) + block, kind)
    edge = pltpu.VMEM((PLANE,) + block, BF16)
    whole = jax.ShapeDtypeStruct((1, sites) + block, F32)
    flops = 2 * count * width * width
    scales = coefficients()

    def with_edges(kernel, outs, operands, edges, flops, name, **more):
        piece = kernel.args[0]
        planes = planes_in(piece)
        old = [p for p in planes if p in edges]
        aliases = {len(operands) + i: len(outs) + planes.index(p) for i, p in enumerate(old)}
        if "in_specs" in more:
            more["in_specs"] = more["in_specs"] + [WHOLE] * len(old)
        outs = call(
            kernel,
            outs + [edge] * len(planes),
            operands + [edges[p] for p in old],
            flops,
            name,
            aliases=aliases,
            **more,
        )
        edges.update(zip(planes, outs[-len(planes) :]))
        return outs[: -len(planes)]

    weight_local, weight_time = prep(self_block, hop_blocks, sites)
    start, sent, edges = [], [], {}
    for i, piece in enumerate(pieces):
        tie = [weight_local[0]] if i == 1 else []
        outs = with_edges(
            functools.partial(first_kernel, piece),
            [vector(piece, BF16)] * 2,
            [residual_in] + tie,
            edges,
            0,
            "first_direction",
            in_specs=[IN_HBM] + [WHOLE] * len(tie),
            scratch=[pltpu.SemaphoreType.DMA((len(piece),))],
        )
        start.append(outs[0])
        sent.append(outs[1])
    residual, direction = start, start
    directions = []
    for number in range(STEPS):
        first, last = number == 0, number == STEPS - 1
        near = [lax.ppermute(v, "site", swap) for v in sent]
        halo = [lax.ppermute(edges[0], "group", chips), lax.ppermute(edges[1], "group", cores)]
        far = [lax.ppermute(v, "site", relay) for v in near]
        acc = [
            call(
                functools.partial(local_kernel, plane, pieces),
                [pltpu.VMEM((PLANE,) + block, F32)],
                [halo[plane], weight_local[plane], *sent, *residual],
                PLANE * 6 * flops,
                "local_terms",
            )[0]
            for plane in range(2)
        ]
        operands = lambda i: [
            *[acc[p] for p in planes_in(pieces[i])],
            *[weight_time[p] for p in planes_in(pieces[i])],
            near[i],
            far[i],
        ]
        if last:
            correction = call(
                functools.partial(sum_kernel, pieces), [whole], [*start, *sum(directions, [])], 0, "correction"
            )[0]
            result = []
            for i, piece in enumerate(pieces):
                known = operands(i)
                result = call(
                    functools.partial(time_kernel, piece, "last", None),
                    [whole],
                    [*known, *result],
                    len(piece) * 2 * flops,
                    "time_terms_last",
                    aliases={len(known): 0} if result else None,
                    in_specs=[WHOLE] * len(known) + [IN_HBM] * len(result),
                    out_specs=[IN_HBM],
                    scratch=[vector(piece, F32), pltpu.SemaphoreType.DMA((len(piece),))],
                )
            return correction, result[0]
        edges = {}
        new = [
            with_edges(
                functools.partial(time_kernel, piece, "first" if first else "middle", scales[number]),
                [vector(piece, F32), vector(piece, F32), vector(piece, BF16)],
                operands(i) + [direction[i]],
                edges,
                len(piece) * 2 * flops,
                "time_terms",
            )
            for i, piece in enumerate(pieces)
        ]
        residual, direction, sent = map(list, zip(*new))
        directions.append(direction)


def solution(mesh):
    return jax.shard_map(
        body,
        mesh=mesh,
        in_specs=(
            P("site", "group", None, None),
            P("site", None, None, None),
            P("site", None, None, None, None),
        ),
        out_specs=(P("site", "group", None, None), P("site", "group", None, None)),
        check_vma=False,
    )
```

```python
import functools

import jax
import jax.numpy as jnp
from jax import lax
from jax.experimental import pallas as pl
from jax.experimental.pallas import tpu as pltpu
from jax.sharding import PartitionSpec as P

LY = 4
LZ = 2
STEPS = 4
PLANE = LY * LZ
PIECES = 3

diagonal_shift = 1.5
center_value = 1.5
half_width = 1.0

F32, BF16 = jnp.float32, jnp.bfloat16
WHOLE = pl.BlockSpec(memory_space=pltpu.VMEM)
IN_HBM = pl.BlockSpec(memory_space=pltpu.HBM)
VMEM_LIMIT = 32 * 1024 * 1024


def coefficients():
    ratio = half_width / center_value
    out = []
    for _ in range(STEPS - 1):
        ratio_next = 1.0 / (2.0 * center_value / half_width - ratio)
        out.append((ratio_next * ratio, 2.0 * ratio_next / half_width))
        ratio = ratio_next
    return out


def call(kernel, outs, operands, flops, name, aliases=None, out_specs=None, in_specs=None, scratch=()):
    nbytes = sum(o.size * o.dtype.itemsize for o in operands)
    in_specs = in_specs or [WHOLE] * len(operands)
    out_specs = out_specs or [WHOLE] * len(outs)
    operands = [
        pltpu.with_memory_space_constraint(o, pltpu.VMEM if s is WHOLE else pltpu.HBM)
        for o, s in zip(operands, in_specs)
    ]
    return pl.pallas_call(
        kernel,
        out_shape=outs,
        in_specs=in_specs,
        out_specs=out_specs,
        input_output_aliases=aliases or {},
        scratch_shapes=scratch,
        compiler_params=pltpu.CompilerParams(vmem_limit_bytes=VMEM_LIMIT),
        cost_estimate=pl.CostEstimate(flops=flops, bytes_accessed=nbytes, transcendentals=0),
        name=name,
    )(*operands)


def odd_group():
    return lax.axis_index("group") % 2


def plane_of(plane):
    return (plane + odd_group()) % 2


def place_of(site):
    return plane_of(site // PLANE) * PLANE + site % PLANE


def real_form(block):
    block = block.astype(F32)
    half = block.shape[-1] // 2
    lane = lax.broadcasted_iota(jnp.int32, block.shape, 1)
    upper = jnp.where(lane < half, block, -block)
    lower = pltpu.roll(block, half, 1)
    return jnp.concatenate([upper, lower], axis=0)


def prep_kernel(batch, self_hbm, hop_hbm, *refs):
    local_refs, time_refs, (self_ref, hop_ref, sems) = refs[:2], refs[2:4], refs[4:]
    sites = hop_ref.shape[0]
    width = local_refs[0].shape[1]
    parity = lax.axis_index("site") % 2
    copies = []
    for i in range(sites // batch):
        piece, offset = divmod(i * batch, PLANE)
        base = lax.axis_index("group") * sites + plane_of(piece) * PLANE + offset
        there, here = pl.ds(pl.multiple_of(base, batch), batch), pl.ds(i * batch, batch)
        copies.append(
            (
                pltpu.make_async_copy(hop_hbm.at[0, there], hop_ref.at[here], sems.at[0, i]),
                pltpu.make_async_copy(self_hbm.at[0, there], self_ref.at[here], sems.at[1, i]),
            )
        )
        for copy in copies[i]:
            copy.start()
    for site in range(sites):
        if site % batch == 0:
            for copy in copies[site // batch]:
                copy.wait()
        piece, own = divmod(site, PLANE)
        plane = plane_of(piece)
        hop = lambda m: real_form(hop_ref[site, m])
        parts = [
            real_form(self_ref[site]),
            hop(plane),
            hop(2),
            hop(3),
            hop(4) + hop(5),
            hop(1 - plane),
        ]
        for k, part in enumerate(parts):
            local_refs[piece][own, :, k * width : (k + 1) * width] = part.astype(BF16)
        time_refs[piece][own, :, :width] = hop(6 + parity).astype(BF16)
        time_refs[piece][own, :, width:] = hop(7 - parity).astype(BF16)


def prep(self_block, hop_blocks, sites):
    comps, width = self_block.shape[2:]
    batch = 2
    weight = lambda parts: pltpu.VMEM((PLANE, width, parts * width), BF16)
    outs = call(
        functools.partial(prep_kernel, batch),
        [weight(6)] * 2 + [weight(2)] * 2,
        [self_block, hop_blocks],
        0,
        "prep",
        in_specs=[IN_HBM, IN_HBM],
        scratch=[
            pltpu.VMEM((sites, comps, width), BF16),
            pltpu.VMEM((sites, 8, comps, width), BF16),
            pltpu.SemaphoreType.DMA((2, sites // batch)),
        ],
    )
    return outs[:2], outs[2:4]


def times(vector, weight):
    return lax.dot_general(
        vector, weight, (((1,), (1,)), ((), ())), preferred_element_type=F32
    )


def planes_in(piece):
    return sorted({site // PLANE for site in piece})


def store_edges(piece, sent_out, edges):
    for plane, edge in zip(planes_in(piece), edges):
        mine = [site for site in piece if site // PLANE == plane]
        edge[pl.ds(mine[0] % PLANE, len(mine))] = sent_out[pl.ds(mine[0] - piece[0], len(mine))]


def first_kernel(piece, residual_hbm, *refs):
    planes = len(planes_in(piece))
    residual, sent_out, *edges, sems = refs[-3 - planes :]
    copies = [
        pltpu.make_async_copy(residual_hbm.at[0, place_of(site)], residual.at[s], sems.at[s])
        for s, site in enumerate(piece)
    ]
    for copy in copies:
        copy.start()
    for s, copy in enumerate(copies):
        copy.wait()
        sent_out[s] = (residual[s].astype(F32) * (half_width / center_value)).astype(BF16)
    store_edges(piece, sent_out, edges)


def local_kernel(plane, pieces, halo, weight, *refs):
    count = len(pieces)
    sent, residual, acc = refs[:count], refs[count : 2 * count], refs[-1]

    def at(of, site):
        piece = max(i for i in range(count) if pieces[i][0] <= site)
        return of[piece][site - pieces[piece][0]]

    for s in range(PLANE):
        y, z = s // LZ, s % LZ
        here = lambda y, z: at(sent, plane * PLANE + y % LY * LZ + z)
        own = here(y, z)
        around = jnp.concatenate(
            [own, at(sent, (1 - plane) * PLANE + s), here(y + 1, z), here(y - 1, z), here(y, 1 - z), halo[s]],
            axis=1,
        )
        acc[s] = (
            at(residual, plane * PLANE + s).astype(F32)
            - diagonal_shift * own.astype(F32)
            - times(around, weight[s])
        )


def time_kernel(piece, mode, scale, *refs):
    planes = planes_in(piece)
    acc, weight = refs[: len(planes)], refs[len(planes) : 2 * len(planes)]
    near, far, *refs = refs[2 * len(planes) :]
    if mode == "last":
        whole, out, sems = refs[-3:]
        copies = [
            pltpu.make_async_copy(out.at[s], whole.at[0, place_of(site)], sems.at[s])
            for s, site in enumerate(piece)
        ]
    else:
        direction = refs[0]
        out, direction_out, sent_out, *edges = refs[-3 - len(planes) :]
    for s, site in enumerate(piece):
        plane = planes.index(site // PLANE)
        around = jnp.concatenate([near[s], far[s]], axis=1)
        now = acc[plane][site % PLANE] - times(around, weight[plane][site % PLANE])
        out[s] = now
        if mode == "last":
            copies[s].start()
            continue
        old = direction[s].astype(F32)
        if mode == "first":
            old = old * (half_width / center_value)
        new = scale[0] * old + scale[1] * now
        direction_out[s] = new
        sent_out[s] = new.astype(BF16)
    if mode == "last":
        for copy in copies:
            copy.wait()
    else:
        store_edges(piece, sent_out, edges)


def pass_kernel(*refs):
    pass


def sum_kernel(pieces, *refs):
    out, count = refs[-1], len(pieces)
    for i, piece in enumerate(pieces):
        for s, site in enumerate(piece):
            total = refs[i][s].astype(F32) * (half_width / center_value)
            for ref in refs[i + count : -1 : count]:
                total = total + ref[s]
            out[0, place_of(site)] = total


def body(residual_in, self_block, hop_blocks):
    _, sites, count, width = residual_in.shape
    groups, slices = lax.axis_size("group"), lax.axis_size("site")
    assert sites == 2 * PLANE and slices % 2 == 0 and groups % 2 == 0
    swap = [(t, t ^ 1) for t in range(slices)]
    relay = [(t, (t + 2 - 4 * (t % 2)) % slices) for t in range(slices)]
    cores = [(i, i ^ 1) for i in range(groups)]
    chips = [(i, (i - 1 + 2 * (i % 2)) % groups) for i in range(groups)]

    block = (count, width)
    offsets = [-(-i * sites // PIECES) for i in range(PIECES + 1)]
    pieces = [tuple(range(a, b)) for a, b in zip(offsets, offsets[1:])]
    vector = lambda piece, kind: pltpu.VMEM((len(piece),) + block, kind)
    edge = pltpu.VMEM((PLANE,) + block, BF16)
    whole = jax.ShapeDtypeStruct((1, sites) + block, F32)
    flops = 2 * count * width * width
    scales = coefficients()

    def with_edges(kernel, outs, operands, edges, flops, name, **more):
        piece = kernel.args[0]
        planes = planes_in(piece)
        old = [p for p in planes if p in edges]
        aliases = {len(operands) + i: len(outs) + planes.index(p) for i, p in enumerate(old)}
        if "in_specs" in more:
            more["in_specs"] = more["in_specs"] + [WHOLE] * len(old)
        outs = call(
            kernel,
            outs + [edge] * len(planes),
            operands + [edges[p] for p in old],
            flops,
            name,
            aliases=aliases,
            **more,
        )
        edges.update(zip(planes, outs[-len(planes) :]))
        return outs[: -len(planes)]

    weight_local, weight_time = prep(self_block, hop_blocks, sites)
    start, sent, edges = [], [], {}
    for i, piece in enumerate(pieces):
        tie = [weight_local[0]] if i == 1 else []
        outs = with_edges(
            functools.partial(first_kernel, piece),
            [vector(piece, BF16)] * 2,
            [residual_in] + tie,
            edges,
            0,
            "first_direction",
            in_specs=[IN_HBM] + [WHOLE] * len(tie),
            scratch=[pltpu.SemaphoreType.DMA((len(piece),))],
        )
        start.append(outs[0])
        sent.append(outs[1])
    residual, direction = start, start
    directions = []
    for number in range(STEPS):
        first, last = number == 0, number == STEPS - 1
        near = [lax.ppermute(v, "site", swap) for v in sent]
        halo = [lax.ppermute(edges[0], "group", chips), lax.ppermute(edges[1], "group", cores)]
        if last:
            correction = call(
                functools.partial(sum_kernel, pieces), [whole], [*start, *sum(directions, [])], 0, "correction"
            )[0]
            near[1] = call(
                pass_kernel,
                [vector(pieces[1], BF16)],
                [near[1], correction],
                0,
                "order",
                aliases={0: 0},
                in_specs=[WHOLE, IN_HBM],
            )[0]
        far = [lax.ppermute(v, "site", relay) for v in near]
        acc = [
            call(
                functools.partial(local_kernel, plane, pieces),
                [pltpu.VMEM((PLANE,) + block, F32)],
                [halo[plane], weight_local[plane], *sent, *residual],
                PLANE * 6 * flops,
                "local_terms",
            )[0]
            for plane in range(2)
        ]
        operands = lambda i: [
            *[acc[p] for p in planes_in(pieces[i])],
            *[weight_time[p] for p in planes_in(pieces[i])],
            near[i],
            far[i],
        ]
        if last:
            result = []
            for i, piece in enumerate(pieces):
                known = operands(i)
                result = call(
                    functools.partial(time_kernel, piece, "last", None),
                    [whole],
                    [*known, *result],
                    len(piece) * 2 * flops,
                    "time_terms_last",
                    aliases={len(known): 0} if result else None,
                    in_specs=[WHOLE] * len(known) + [IN_HBM] * len(result),
                    out_specs=[IN_HBM],
                    scratch=[vector(piece, F32), pltpu.SemaphoreType.DMA((len(piece),))],
                )
            return correction, result[0]
        edges = {}
        new = [
            with_edges(
                functools.partial(time_kernel, piece, "first" if first else "middle", scales[number]),
                [vector(piece, F32), vector(piece, F32), vector(piece, BF16)],
                operands(i) + [direction[i]],
                edges,
                len(piece) * 2 * flops,
                "time_terms",
            )
            for i, piece in enumerate(pieces)
        ]
        residual, direction, sent = map(list, zip(*new))
        directions.append(direction)


def solution(mesh):
    return jax.shard_map(
        body,
        mesh=mesh,
        in_specs=(
            P("site", "group", None, None),
            P("site", None, None, None),
            P("site", None, None, None, None),
        ),
        out_specs=(P("site", "group", None, None), P("site", "group", None, None)),
        check_vma=False,
    )
```

```python
import functools

import jax
import jax.numpy as jnp
from jax import lax
from jax.experimental import pallas as pl
from jax.experimental.pallas import tpu as pltpu
from jax.sharding import PartitionSpec as P

LY = 4
LZ = 2
STEPS = 4
PLANE = LY * LZ
PIECES = 3

diagonal_shift = 1.5
center_value = 1.5
half_width = 1.0

F32, BF16 = jnp.float32, jnp.bfloat16
WHOLE = pl.BlockSpec(memory_space=pltpu.VMEM)
IN_HBM = pl.BlockSpec(memory_space=pltpu.HBM)
VMEM_LIMIT = 32 * 1024 * 1024


def coefficients():
    ratio = half_width / center_value
    out = []
    for _ in range(STEPS - 1):
        ratio_next = 1.0 / (2.0 * center_value / half_width - ratio)
        out.append((ratio_next * ratio, 2.0 * ratio_next / half_width))
        ratio = ratio_next
    return out


def call(kernel, outs, operands, flops, name, aliases=None, out_specs=None, in_specs=None, scratch=()):
    nbytes = sum(o.size * o.dtype.itemsize for o in operands)
    in_specs = in_specs or [WHOLE] * len(operands)
    out_specs = out_specs or [WHOLE] * len(outs)
    operands = [
        pltpu.with_memory_space_constraint(o, pltpu.VMEM if s is WHOLE else pltpu.HBM)
        for o, s in zip(operands, in_specs)
    ]
    return pl.pallas_call(
        kernel,
        out_shape=outs,
        in_specs=in_specs,
        out_specs=out_specs,
        input_output_aliases=aliases or {},
        scratch_shapes=scratch,
        compiler_params=pltpu.CompilerParams(vmem_limit_bytes=VMEM_LIMIT),
        cost_estimate=pl.CostEstimate(flops=flops, bytes_accessed=nbytes, transcendentals=0),
        name=name,
    )(*operands)


def odd_group():
    return lax.axis_index("group") % 2


def plane_of(plane):
    return (plane + odd_group()) % 2


def place_of(site):
    return plane_of(site // PLANE) * PLANE + site % PLANE


def real_form(block):
    block = block.astype(F32)
    half = block.shape[-1] // 2
    lane = lax.broadcasted_iota(jnp.int32, block.shape, 1)
    upper = jnp.where(lane < half, block, -block)
    lower = pltpu.roll(block, half, 1)
    return jnp.concatenate([upper, lower], axis=0)


def prep_kernel(batch, self_hbm, hop_hbm, *refs):
    local_refs, time_refs, (self_ref, hop_ref, sems) = refs[:2], refs[2:4], refs[4:]
    sites = hop_ref.shape[0]
    width = local_refs[0].shape[1]
    parity = lax.axis_index("site") % 2
    copies = []
    for i in range(sites // batch):
        piece, offset = divmod(i * batch, PLANE)
        base = lax.axis_index("group") * sites + plane_of(piece) * PLANE + offset
        there, here = pl.ds(pl.multiple_of(base, batch), batch), pl.ds(i * batch, batch)
        copies.append(
            (
                pltpu.make_async_copy(hop_hbm.at[0, there], hop_ref.at[here], sems.at[0, i]),
                pltpu.make_async_copy(self_hbm.at[0, there], self_ref.at[here], sems.at[1, i]),
            )
        )
        for copy in copies[i]:
            copy.start()
    for site in range(sites):
        if site % batch == 0:
            for copy in copies[site // batch]:
                copy.wait()
        piece, own = divmod(site, PLANE)
        plane = plane_of(piece)
        hop = lambda m: real_form(hop_ref[site, m])
        parts = [
            real_form(self_ref[site]),
            hop(plane),
            hop(2),
            hop(3),
            hop(4) + hop(5),
            hop(1 - plane),
        ]
        for k, part in enumerate(parts):
            local_refs[piece][own, :, k * width : (k + 1) * width] = part.astype(BF16)
        time_refs[piece][own, :, :width] = hop(6 + parity).astype(BF16)
        time_refs[piece][own, :, width:] = hop(7 - parity).astype(BF16)


def prep(self_block, hop_blocks, sites):
    comps, width = self_block.shape[2:]
    batch = 2
    weight = lambda parts: pltpu.VMEM((PLANE, width, parts * width), BF16)
    outs = call(
        functools.partial(prep_kernel, batch),
        [weight(6)] * 2 + [weight(2)] * 2,
        [self_block, hop_blocks],
        0,
        "prep",
        in_specs=[IN_HBM, IN_HBM],
        scratch=[
            pltpu.VMEM((sites, comps, width), BF16),
            pltpu.VMEM((sites, 8, comps, width), BF16),
            pltpu.SemaphoreType.DMA((2, sites // batch)),
        ],
    )
    return outs[:2], outs[2:4]


def times(vector, weight):
    return lax.dot_general(
        vector, weight, (((1,), (1,)), ((), ())), preferred_element_type=F32
    )


def planes_in(piece):
    return sorted({site // PLANE for site in piece})


def store_edges(piece, sent_out, edges):
    for plane, edge in zip(planes_in(piece), edges):
        mine = [site for site in piece if site // PLANE == plane]
        edge[pl.ds(mine[0] % PLANE, len(mine))] = sent_out[pl.ds(mine[0] - piece[0], len(mine))]


def first_kernel(pieces, residual_hbm, *refs):
    out, sems = refs[:-1], refs[-1]
    copies = [
        pltpu.make_async_copy(residual_hbm.at[0, place_of(site)], out[i].at[s], sems.at[site])
        for i, piece in enumerate(pieces)
        for s, site in enumerate(piece)
    ]
    for copy in copies:
        copy.start()
    for copy in copies:
        copy.wait()


def direction_kernel(piece, residual, *refs):
    sent_out, *edges = refs[-1 - len(planes_in(piece)) :]
    for s in range(len(piece)):
        sent_out[s] = (residual[s].astype(F32) * (half_width / center_value)).astype(BF16)
    store_edges(piece, sent_out, edges)


def local_kernel(plane, pieces, halo, weight, *refs):
    count = len(pieces)
    sent, residual, acc = refs[:count], refs[count : 2 * count], refs[-1]

    def at(of, site):
        piece = max(i for i in range(count) if pieces[i][0] <= site)
        return of[piece][site - pieces[piece][0]]

    for s in range(PLANE):
        y, z = s // LZ, s % LZ
        here = lambda y, z: at(sent, plane * PLANE + y % LY * LZ + z)
        own = here(y, z)
        around = jnp.concatenate(
            [own, at(sent, (1 - plane) * PLANE + s), here(y + 1, z), here(y - 1, z), here(y, 1 - z), halo[s]],
            axis=1,
        )
        acc[s] = (
            at(residual, plane * PLANE + s).astype(F32)
            - diagonal_shift * own.astype(F32)
            - times(around, weight[s])
        )


def time_kernel(piece, mode, scale, *refs):
    planes = planes_in(piece)
    acc, weight = refs[: len(planes)], refs[len(planes) : 2 * len(planes)]
    near, far, *refs = refs[2 * len(planes) :]
    if mode == "last":
        whole, out, sems = refs[-3:]
        copies = [
            pltpu.make_async_copy(out.at[s], whole.at[0, place_of(site)], sems.at[s])
            for s, site in enumerate(piece)
        ]
    else:
        direction = refs[0]
        out, direction_out, sent_out, *edges = refs[-3 - len(planes) :]
    for s, site in enumerate(piece):
        plane = planes.index(site // PLANE)
        around = jnp.concatenate([near[s], far[s]], axis=1)
        now = acc[plane][site % PLANE] - times(around, weight[plane][site % PLANE])
        out[s] = now
        if mode == "last":
            copies[s].start()
            continue
        old = direction[s].astype(F32)
        if mode == "first":
            old = old * (half_width / center_value)
        new = scale[0] * old + scale[1] * now
        direction_out[s] = new
        sent_out[s] = new.astype(BF16)
    if mode == "last":
        for copy in copies:
            copy.wait()
    else:
        store_edges(piece, sent_out, edges)


def sum_kernel(pieces, *refs):
    out, count = refs[-1], len(pieces)
    for i, piece in enumerate(pieces):
        for s, site in enumerate(piece):
            total = refs[i][s].astype(F32) * (half_width / center_value)
            for ref in refs[i + count : -1 : count]:
                total = total + ref[s]
            out[0, place_of(site)] = total


def body(residual_in, self_block, hop_blocks):
    _, sites, count, width = residual_in.shape
    groups, slices = lax.axis_size("group"), lax.axis_size("site")
    assert sites == 2 * PLANE and slices % 2 == 0 and groups % 2 == 0
    swap = [(t, t ^ 1) for t in range(slices)]
    relay = [(t, (t + 2 - 4 * (t % 2)) % slices) for t in range(slices)]
    cores = [(i, i ^ 1) for i in range(groups)]
    chips = [(i, (i - 1 + 2 * (i % 2)) % groups) for i in range(groups)]

    block = (count, width)
    offsets = [-(-i * sites // PIECES) for i in range(PIECES + 1)]
    pieces = [tuple(range(a, b)) for a, b in zip(offsets, offsets[1:])]
    vector = lambda piece, kind: pltpu.VMEM((len(piece),) + block, kind)
    edge = pltpu.VMEM((PLANE,) + block, BF16)
    whole = jax.ShapeDtypeStruct((1, sites) + block, F32)
    flops = 2 * count * width * width
    scales = coefficients()

    def with_edges(kernel, outs, operands, edges, flops, name, **more):
        piece = kernel.args[0]
        planes = planes_in(piece)
        old = [p for p in planes if p in edges]
        aliases = {len(operands) + i: len(outs) + planes.index(p) for i, p in enumerate(old)}
        if "in_specs" in more:
            more["in_specs"] = more["in_specs"] + [WHOLE] * len(old)
        outs = call(
            kernel,
            outs + [edge] * len(planes),
            operands + [edges[p] for p in old],
            flops,
            name,
            aliases=aliases,
            **more,
        )
        edges.update(zip(planes, outs[-len(planes) :]))
        return outs[: -len(planes)]

    weight_local, weight_time = prep(self_block, hop_blocks, sites)
    start = call(
        functools.partial(first_kernel, pieces),
        [vector(piece, BF16) for piece in pieces],
        [residual_in],
        0,
        "residual",
        in_specs=[IN_HBM],
        scratch=[pltpu.SemaphoreType.DMA((sites,))],
    )
    sent, edges = [], {}
    for i, piece in enumerate(pieces):
        tie = [weight_local[0]] if i == 1 else []
        sent += with_edges(
            functools.partial(direction_kernel, piece),
            [vector(piece, BF16)],
            [start[i]] + tie,
            edges,
            0,
            "first_direction",
        )
    residual, direction = start, start
    directions = []
    for number in range(STEPS):
        first, last = number == 0, number == STEPS - 1
        near = [lax.ppermute(v, "site", swap) for v in sent]
        halo = [lax.ppermute(edges[0], "group", chips), lax.ppermute(edges[1], "group", cores)]
        far = [lax.ppermute(v, "site", relay) for v in near]
        acc = [
            call(
                functools.partial(local_kernel, plane, pieces),
                [pltpu.VMEM((PLANE,) + block, F32)],
                [halo[plane], weight_local[plane], *sent, *residual],
                PLANE * 6 * flops,
                "local_terms",
            )[0]
            for plane in range(2)
        ]
        operands = lambda i: [
            *[acc[p] for p in planes_in(pieces[i])],
            *[weight_time[p] for p in planes_in(pieces[i])],
            near[i],
            far[i],
        ]
        if last:
            correction = call(
                functools.partial(sum_kernel, pieces), [whole], [*start, *sum(directions, [])], 0, "correction"
            )[0]
            result = []
            for i, piece in enumerate(pieces):
                known = operands(i)
                result = call(
                    functools.partial(time_kernel, piece, "last", None),
                    [whole],
                    [*known, *result],
                    len(piece) * 2 * flops,
                    "time_terms_last",
                    aliases={len(known): 0} if result else None,
                    in_specs=[WHOLE] * len(known) + [IN_HBM] * len(result),
                    out_specs=[IN_HBM],
                    scratch=[vector(piece, F32), pltpu.SemaphoreType.DMA((len(piece),))],
                )
            return correction, result[0]
        edges = {}
        new = [
            with_edges(
                functools.partial(time_kernel, piece, "first" if first else "middle", scales[number]),
                [vector(piece, F32), vector(piece, F32), vector(piece, BF16)],
                operands(i) + [direction[i]],
                edges,
                len(piece) * 2 * flops,
                "time_terms",
            )
            for i, piece in enumerate(pieces)
        ]
        residual, direction, sent = map(list, zip(*new))
        directions.append(direction)


def solution(mesh):
    return jax.shard_map(
        body,
        mesh=mesh,
        in_specs=(
            P("site", "group", None, None),
            P("site", None, None, None),
            P("site", None, None, None, None),
        ),
        out_specs=(P("site", "group", None, None), P("site", "group", None, None)),
        check_vma=False,
    )
```
